128 devices in a mesh: row: 16 (over y, z), col: 8 (over x, core).
Axes of the slice: x: 4, y: 4, z: 4, core: 2. Of those that a mesh axis runs over, the one named last changes fastest.
Arguments:
- front: float32 [8192, 8192], P('row', 'col'), may hold values from -25.5 to 328.81723, as said below
- child_tiles: float32 [16, 64, 512, 512], P('row', 'col'), may hold values from -3 to 3
- child_target: int32 [16, 64, 2], P('row', 'col'), may hold values from 0 to 15, as said below
- child_count: int32 [16, 8], P('row', 'col'), may hold values from 6 to 8
Outputs:
- panel: float32 [8192, 2048], P('row')
- updated: float32 [8192, 8192], P('row', 'col')
The draws below stay inside these ranges and needn't reach their ends.
Inputs may be any that keep to these rules, and one draw needn't show every extreme that they name: front is symmetric, and the leading 4 * 512 by 2048 block of assembled is positive definite. `child_target`: within the slots of one device (i, j), the row tiles r have distinct grid rows r; every column tile c satisfies c // 2 = j.
All inputs are finite; a program needn't handle non-finite values.
Results may differ from the reference program's by a relative error of at most 0.0003.
Values sent between devices are 32-bit elements; how exact they have to be, the bound alone decides.
A program may use at most 256 MiB of HBM per device.

```python
import math
import jax
import jax.numpy as jnp
from jax import lax

B = 512
F = 8192
NP = 4
CT = 8
N_ROW = 16
N_COL = 8


def draw_front(key, part):
    key = jax.random.fold_in(key, 11)
    first_key, lead_key, trail_key = jax.random.split(key, 3)
    leading = NP * B
    raw = jnp.clip(jax.random.normal(first_key, (F, F), jnp.float32), -6.0, 6.0)
    strength = 4.0
    mirrored = (raw + raw.T) * 0.70710677
    inside = jnp.arange(F) < leading
    crossing = inside[:, None] != inside[None, :]
    scaled = jnp.where(crossing, 3.0 * mirrored, mirrored)
    bound = math.sqrt((4 + N_ROW) * leading)
    lead_diag = jnp.exp(jax.random.uniform(lead_key, (F,), jnp.float32, math.log(1.2), math.log(1.59))) * bound
    trail_diag = jnp.exp(jax.random.uniform(trail_key, (F,), jnp.float32, math.log(2.5), math.log(4.9))) * math.sqrt(leading)
    diagonal = jnp.where(inside, lead_diag, trail_diag)
    positions = jnp.arange(F, dtype=jnp.int32)
    on_diag = positions[:, None] == positions[None, :]
    distance = jnp.abs(positions[:, None] - positions[None, :]).astype(jnp.float32)
    both_inside = inside[:, None] & inside[None, :]
    smooth = jnp.where(both_inside, strength * jnp.exp(-distance / float(leading)), 0.0)
    return (jnp.where(on_diag, diagonal[None, :], scaled) + smooth).astype(jnp.float32)


def draw_child_tiles(key, part):
    key = jax.random.fold_in(key, 5)
    shape = (N_ROW, N_COL * CT, B, B)
    values = jnp.clip(jax.random.normal(key, shape, jnp.float32), -6.0, 6.0) * 0.5
    return values.astype(jnp.float32)


def draw_child_target(key, part):
    key = jax.random.fold_in(key, 23)
    order_key, row_key, col_key = jax.random.split(key, 3)
    rows_per = F // (B * N_ROW)
    cols_per = F // (B * N_COL)
    scores = jax.random.randint(order_key, (N_ROW, N_COL, N_ROW), 0, 1 << 20) * N_ROW + jnp.arange(N_ROW)
    ranking = jnp.argsort(scores, axis=-1)
    owners = ranking[:, :, :CT]
    row_tiles = owners * rows_per + jax.random.randint(row_key, (N_ROW, N_COL, CT), 0, rows_per)
    base_col = jnp.arange(N_COL)[None, :, None] * cols_per
    col_tiles = base_col + jax.random.randint(col_key, (N_ROW, N_COL, CT), 0, cols_per)
    col_tiles = jnp.minimum(col_tiles, jnp.maximum(row_tiles, base_col))
    paired = jnp.stack([row_tiles, col_tiles], axis=-1)
    return paired.reshape(N_ROW, N_COL * CT, 2).astype(jnp.int32)


def draw_child_count(key, part):
    key = jax.random.fold_in(key, 37)
    dropped = jax.random.randint(key, (N_ROW, N_COL), 0, 3)
    counts = jnp.maximum(CT - dropped, 1)
    corner = jnp.arange(N_ROW)[:, None] + jnp.arange(N_COL)[None, :] == 0
    return jnp.where(corner, CT, counts).astype(jnp.int32)


def setup_inputs(seed: int = 0) -> dict:
    seeds = jax.random.split(jax.random.key(seed), 5)
    front = draw_front(jax.random.fold_in(seeds[4], 71), 0)
    child_tiles = draw_child_tiles(jax.random.fold_in(seeds[4], 71), 0)
    child_target = draw_child_target(jax.random.fold_in(seeds[4], 71), 0)
    child_count = draw_child_count(jax.random.fold_in(seeds[4], 71), 0)
    return {"front": front, "child_tiles": child_tiles, "child_target": child_target, "child_count": child_count}


def symmetric_tile(block):
    return jnp.tril(block) + jnp.tril(block, -1).T

def reference(front, child_tiles, child_target, child_count):
    tiles_side = F // B
    slot_count = child_tiles.shape[1]
    per_device = slot_count // N_COL
    slot_ids = jnp.arange(slot_count, dtype=jnp.int32)
    blocked = front.reshape(tiles_side, B, tiles_side, B)

    def add_row(index, acc):
        tiles_here = child_tiles[index]
        counts_here = child_count[index][slot_ids // per_device]
        live_here = slot_ids % per_device < counts_here
        taken = jnp.where(live_here[:, None, None], tiles_here, jnp.zeros_like(tiles_here))
        row_tile = child_target[index, :, 0]
        col_tile = child_target[index, :, 1]
        return acc.at[row_tile, :, col_tile, :].add(taken)
    blocked = lax.fori_loop(0, N_ROW, add_row, blocked)
    assembled = blocked.reshape(F, F)
    row_tile_of = jnp.arange(F, dtype=jnp.int32) // B
    strip_width = NP * B
    work_strip = assembled[:, :strip_width]
    columns = []
    for panel_index in range(NP):
        first_col = panel_index * B
        factor = jnp.linalg.cholesky(symmetric_tile(work_strip[first_col:first_col + B, first_col:first_col + B]))
        strip_now = work_strip[:, first_col:first_col + B]
        solved = lax.linalg.triangular_solve(factor, strip_now, left_side=False, lower=True, transpose_a=True)
        column = jnp.where(row_tile_of[:, None] > panel_index, solved, jnp.zeros_like(solved))
        column = jnp.where(row_tile_of[:, None] == panel_index, jnp.tile(factor, (tiles_side, 1)), column)
        if panel_index + 1 < NP:
            following = column[first_col + B:strip_width]
            target_cols = work_strip[:, first_col + B:strip_width]
            fresh = target_cols - jnp.dot(column, following.T, precision=lax.Precision.HIGHEST)
            work_strip = work_strip.at[:, first_col + B:strip_width].set(fresh)
        columns.append(column)
    panel = jnp.concatenate(columns, axis=1)
    updated = assembled - jnp.dot(panel, panel.T, precision=lax.Precision.HIGHEST)
    return (panel, updated)
```

```python
import functools
import jax
import jax.numpy as jnp
from jax import lax
from jax.experimental import pallas as pl
from jax.experimental.pallas import tpu as pltpu

MESH = pl.DeviceIdType.MESH
ROWS = 16
CHUNK = 32


def lb(x,j): return jnp.broadcast_to(x[:,j:j+1],x.shape)
def sb(x,s): return jnp.broadcast_to(x[s:s+1,:],x.shape)
def chol128(D,E,M=8,n=128):
    sub = lax.broadcasted_iota(jnp.int32,(8,128),0)
    G=len(D)
    for g in range(G):
        for m0 in range(0,8,M):
            base=8*g+m0
            C=[lb(D[g],base+c) for c in range(M)]
            a=[[sb(C[c],m0+r) if c<=r else None for c in range(M)] for r in range(M)]
            U=[];V=[];R=[]
            l=[[None]*M for _ in range(M)]
            for k in range(M):
                rk=lax.rsqrt(a[k][k]); R.append(rk)
                for i in range(k+1,M): l[i][k]=a[i][k]*rk
                for i in range(k+1,M):
                    for c in range(k+1,i+1):
                        a[i][c]=a[i][c]-l[i][k]*l[c][k]
            for k in range(M):
                u=sb(D[g],m0+k); v=sb(E[g],m0+k)
                for c in range(k):
                    u=u-l[k][c]*U[c]; v=v-l[k][c]*V[c]
                U.append(u*R[k]); V.append(v*R[k])
            for h in range(g,G):
                if h==g and m0+M>=8: continue
                Ch=C if h==g else [lb(D[h],base+c) for c in range(M)]
                L=[]
                for k in range(M):
                    x=Ch[k]
                    for c in range(k): x=x-L[c]*l[k][c]
                    L.append(x*R[k])
                d=D[h]; e=E[h]
                for k in range(M):
                    lk=jnp.where(sub>=m0+M,L[k],0.0) if h==g else L[k]
                    d=d-lk*U[k]; e=e-lk*V[k]
                D[h]=d;E[h]=e
            for k in range(M):
                D[g]=jnp.where(sub==m0+k,U[k],D[g]); E[g]=jnp.where(sub==m0+k,V[k],E[g])
    return D,E

B=512;S=128

HI=lax.Precision.HIGHEST; H3=lax.Precision.HIGH
def dot_nt(a,b,prec): return lax.dot_general(a,b,(((1,),(1,)),((),())),precision=prec,preferred_element_type=jnp.float32)
def dot_nn(a,b,prec): return lax.dot_general(a,b,(((1,),(0,)),((),())),precision=prec,preferred_element_type=jnp.float32)

def factor_tile(w, ti, base):
    r=lambda b: pl.ds(pl.multiple_of(base+b*S,S),S)
    eye=[(lax.broadcasted_iota(jnp.int32,(8,S),0)+8*g==lax.broadcasted_iota(jnp.int32,(8,S),1)).astype(jnp.float32) for g in range(16)]
    row=lax.broadcasted_iota(jnp.int32,(S,S),0); col=lax.broadcasted_iota(jnp.int32,(S,S),1)
    lowm=row>=col
    nb=B//S
    T={}
    for i in range(nb):
        for j in range(i+1):
            x=w[r(i),r(j)]
            if i==j:
                x=jnp.where(lowm,x,x.T)
            T[i,j]=x
    inv={}
    for b in range(nb):
        x=T[b,b]
        D,E=chol128([x[8*g:8*g+8] for g in range(16)],list(eye))
        U=jnp.concatenate(D,0); I=jnp.concatenate(E,0)
        I=jnp.where(lowm,I,0.0)
        w[r(b),r(b)]=jnp.where(lowm,U.T,0.0)
        inv[b,b]=I
        for i in range(b+1,nb):
            P=dot_nt(T[i,b],I,HI)
            T[i,b]=P
            w[r(i),r(b)]=P
            w[r(b),r(i)]=jnp.zeros((S,S),jnp.float32)
        for i in range(b+1,nb):
            for j in range(b+1,i+1):
                T[i,j]=T[i,j]-dot_nt(T[i,b],T[j,b],HI)
        for j in range(b):
            acc=None
            for k in range(j,b):
                t=dot_nn(T[b,k],inv[k,j],HI)
                acc=t if acc is None else acc+t
            inv[b,j]=-dot_nn(I,acc,HI)
        for j in range(nb):
            ti[b*S:(b+1)*S,j*S:(j+1)*S]=inv[b,j] if j<=b else jnp.zeros((S,S),jnp.float32)

def kern(w,ti):
    w[...]=(lax.broadcasted_iota(jnp.int32,(2048,2048),0)==lax.broadcasted_iota(jnp.int32,(2048,2048),1)).astype(jnp.float32)
    zero=jnp.zeros((B,B),jnp.float32)
    def tile(p,c):
        base=pl.multiple_of(p*B,B)
        factor_tile(w,ti.at[p],base)
        def solve(q,c):
            o=pl.ds(pl.multiple_of(q*B,B),B)
            w[o,pl.ds(base,B)]=dot_nt(w[o,pl.ds(base,B)],ti[p],H3)
            return c
        lax.fori_loop(p+1,4,solve,0)
        def upd(q,c):
            o=pl.ds(pl.multiple_of(q*B,B),B)
            w[pl.ds(base,B),o]=zero
            def inner(s,c):
                o2=pl.ds(pl.multiple_of(s*B,B),B)
                w[o,o2]=w[o,o2]-dot_nt(w[o,pl.ds(base,B)],w[o2,pl.ds(base,B)],H3)
                return c
            return lax.fori_loop(p+1,q+1,inner,c)
        lax.fori_loop(p+1,4,upd,0)
        return c
    lax.fori_loop(0,4,tile,0)


def ext_kernel(child, front, meta, out, recv1, send2, recv2, meta_all, meta_s, s1, r1, s2, r2, sm, rm, lsem, w, ti):
    me = lax.axis_index("row")
    col = lax.axis_index("col")
    y, z = me // 4, me % 4
    barrier = pltpu.get_barrier_semaphore()

    def peer(o):
        dy, dz = o // 4, o % 4
        return (y + dy) % 4 * 4 + (z + dz) % 4

    def source(o):
        dy, dz = o // 4, o % 4
        return (y + 4 - dy) % 4 * 4 + (z + 4 - dz) % 4

    order = [10, 9, 11, 6, 14, 5, 7, 13, 15, 2, 8, 1, 3, 4, 12]
    for o in order:
        pl.semaphore_signal(barrier, inc=1, device_id=(peer(o), col), device_id_type=MESH)
    pl.semaphore_wait(barrier, len(order))

    def meta_copy(o):
        return pltpu.make_async_remote_copy(meta, meta_all.at[me], sm.at[o], rm.at[o], device_id=(peer(o), col), device_id_type=MESH)

    def chunk_copy(o):
        rows = pl.ds(pl.multiple_of(peer(o) * CHUNK, CHUNK), CHUNK)
        return pltpu.make_async_remote_copy(child.at[0, :, rows, :], recv1.at[me], s1.at[o], r1.at[o], device_id=(peer(o), col), device_id_type=MESH)

    for o in order:
        meta_copy(o).start()
    for o in order:
        chunk_copy(o).start()
    rows_me = pl.ds(pl.multiple_of(me * CHUNK, CHUNK), CHUNK)
    own = pltpu.make_async_copy(child.at[0, :, rows_me, :], recv1.at[me], lsem.at[0])
    own.start()
    own_meta = pltpu.make_async_copy(meta, meta_all.at[me], lsem.at[1])
    own_meta.start()
    own.wait()
    own_meta.wait()
    for o in order:
        meta_copy(o).wait()
    to_smem = pltpu.make_async_copy(meta_all, meta_s, lsem.at[2])
    to_smem.start()
    to_smem.wait()
    kern(w,ti)
    for o in order:
        chunk_copy(o).wait()

    def reduce_for(d):
        def step(i, acc):
            slot = meta_s[i, 0, d]
            code = meta_s[i, 1, d]
            value = recv1[i, slot]
            first = jnp.where(code == 0, 1.0, 0.0)
            second = jnp.where(code == 1, 1.0, 0.0)
            return acc[0] + value * first, acc[1] + value * second

        zero = jnp.zeros((CHUNK, 512), jnp.float32)
        a, b = lax.fori_loop(0, ROWS, step, (zero, zero))
        send2[d, :, 0:512] = a
        send2[d, :, 512:1024] = b

    def sum_copy(o):
        return pltpu.make_async_remote_copy(send2.at[peer(o)], recv2.at[me], s2.at[o], r2.at[o], device_id=(peer(o), col), device_id_type=MESH)

    for o in order:
        reduce_for(peer(o))
        sum_copy(o).start()
    reduce_for(me)
    recv2[me] = send2[me]
    for o in order:
        sum_copy(o).wait()
    out[...] = front[...] + recv2[...].reshape(512, 1024) + (w[0:512,0:1024]-w[512:1024,0:1024])*0.0


def extend_add(front, child_tiles, meta):
    return pl.pallas_call(
        ext_kernel,
        out_shape=jax.ShapeDtypeStruct((512, 1024), jnp.float32),
        in_specs=[pl.BlockSpec(memory_space=pl.ANY), pl.BlockSpec(memory_space=pltpu.VMEM), pl.BlockSpec(memory_space=pltpu.VMEM)],
        out_specs=pl.BlockSpec(memory_space=pltpu.VMEM),
        scratch_shapes=[
            pltpu.VMEM((ROWS, 8, CHUNK, 512), jnp.float32),
            pltpu.VMEM((ROWS, CHUNK, 1024), jnp.float32),
            pltpu.VMEM((ROWS, CHUNK, 1024), jnp.float32),
            pltpu.VMEM((ROWS, 8, 128), jnp.int32),
            pltpu.SMEM((ROWS, 8, 128), jnp.int32),
            pltpu.SemaphoreType.DMA((16,)),
            pltpu.SemaphoreType.DMA((16,)),
            pltpu.SemaphoreType.DMA((16,)),
            pltpu.SemaphoreType.DMA((16,)),
            pltpu.SemaphoreType.DMA((16,)),
            pltpu.SemaphoreType.DMA((16,)),
            pltpu.SemaphoreType.DMA((3,)),
pltpu.VMEM((2048,2048),jnp.float32),pltpu.VMEM((4,512,512),jnp.float32),
        ],
        compiler_params=pltpu.CompilerParams(collective_id=0, has_side_effects=True, vmem_limit_bytes=50 * 2**20),
    )(child_tiles, front, meta)


def make_meta(child_target, child_count):
    targets = child_target.reshape(8, 2)
    live = jnp.arange(8, dtype=jnp.int32) < child_count.reshape(())
    owner = targets[:, 0]
    code = targets[:, 1] % 2
    hit = (owner[:, None] == jnp.arange(16)[None, :]) & live[:, None]
    any_hit = hit.any(axis=0)
    slot = jnp.sum(jnp.where(hit, jnp.arange(8, dtype=jnp.int32)[:, None], 0), axis=0)
    codes = jnp.where(any_hit, jnp.sum(jnp.where(hit, code[:, None], 0), axis=0), 2)
    table = jnp.stack([slot, codes]).astype(jnp.int32)
    return jnp.pad(table, ((0, 6), (0, 112)))

from jax.sharding import PartitionSpec as P
NP = 4


def broadcast(array, axis, root):
    mine = lax.axis_index(axis) == root
    return lax.psum(jnp.where(mine, array, jnp.zeros_like(array)), axis)


def symmetric_tile(block):
    return jnp.tril(block) + jnp.tril(block, -1).T


def body(front, child_tiles, child_target, child_count):
    precise = lax.Precision.HIGHEST
    tile_size = child_tiles.shape[-1]
    row_tiles = front.shape[0] // tile_size
    col_tiles = front.shape[1] // tile_size
    slot_count = child_tiles.shape[1]
    tiles_here = child_tiles.reshape(slot_count, tile_size, tile_size)
    my_row = lax.axis_index('row')
    my_col = lax.axis_index('col')
    assembled = extend_add(front, child_tiles, make_meta(child_target, child_count))
    local_cols = front.shape[1]
    strip_width = NP * tile_size
    strip_calls = max(1, strip_width // local_cols)
    strip_pieces = [broadcast(assembled, "col", owner_col) for owner_col in range(strip_calls)]
    work_strip = jnp.concatenate(strip_pieces, axis=1)
    row_share = col_tiles // row_tiles
    global_tile = (
        my_row * row_tiles + jnp.arange(row_tiles * tile_size, dtype=jnp.int32) // tile_size
    )
    result = assembled
    columns = []
    for panel_index in range(NP):
        first_col = panel_index * tile_size
        within = panel_index % row_tiles * tile_size
        diag_local = work_strip[within : within + tile_size, first_col : first_col + tile_size]
        factor = broadcast(
            jnp.linalg.cholesky(symmetric_tile(diag_local)), "row", panel_index // row_tiles
        )
        strip_now = work_strip[:, first_col : first_col + tile_size]
        solved = lax.linalg.triangular_solve(
            factor, strip_now, left_side=False, lower=True, transpose_a=True
        )
        column = jnp.where(global_tile[:, None] > panel_index, solved, jnp.zeros_like(solved))
        column = jnp.where(
            global_tile[:, None] == panel_index, jnp.tile(factor, (row_tiles, 1)), column
        )
        if panel_index + 1 < NP:
            following_parts = []
            for later in range(panel_index + 1, NP):
                following_parts.append(broadcast(column, "row", later // row_tiles))
            following = jnp.concatenate(following_parts, axis=0)
            target_cols = work_strip[:, first_col + tile_size : strip_width]
            fresh = target_cols - jnp.dot(column, following.T, precision=precise)
            work_strip = work_strip.at[:, first_col + tile_size : strip_width].set(fresh)
        columns.append(column)
    panel = jnp.concatenate(columns, axis=1)
    row_parts = [
        broadcast(panel, "row", my_col * row_share + offset) for offset in range(row_share)
    ]
    result = result - jnp.dot(panel, jnp.concatenate(row_parts, axis=0).T, precision=precise)
    return (panel, result)


def solution(mesh):
    return jax.shard_map(
        body,
        mesh=mesh,
        in_specs=(
            P("row", "col"),
            P("row", "col", None, None),
            P("row", "col", None),
            P("row", "col"),
        ),
        out_specs=(P("row", None), P("row", "col")),
        check_vma=False,
    )
```

```python
import jax
import jax.numpy as jnp
from jax import lax
from jax.experimental import pallas as pl
from jax.experimental.pallas import tpu as pltpu
from jax.sharding import PartitionSpec as P

MESH = pl.DeviceIdType.MESH
F32 = jnp.float32
HIGHEST = lax.Precision.HIGHEST
HIGH = lax.Precision.HIGH
ROWS = 16
CT = 8
B = 512
S = 128
NP = 4
CHUNK = 32
MICRO = 8
NB = B // S
ORDER = (10, 9, 11, 6, 14, 5, 7, 13, 15, 2, 8, 1, 3, 4, 12)
PIECES = (
    (0, 0, 0, 512),
    (0, 1, 0, 1024),
    (0, 2, 0, 1024),
    (0, 3, 0, 1024),
    (1, 2, 1024, 512),
    (1, 3, 1024, 1024),
)


def dot_nt(a, b, precision):
    return lax.dot_general(
        a, b, (((1,), (1,)), ((), ())), precision=precision, preferred_element_type=F32
    )


def dot_nn(a, b, precision):
    return lax.dot_general(
        a, b, (((1,), (0,)), ((), ())), precision=precision, preferred_element_type=F32
    )


def lane(x, j):
    return jnp.broadcast_to(x[:, j : j + 1], x.shape)


def sublane(x, s):
    return jnp.broadcast_to(x[s : s + 1, :], x.shape)


def eliminate(d, e):
    groups = len(d)
    for g in range(groups):
        base = MICRO * g
        cols = [lane(d[g], base + c) for c in range(MICRO)]
        a = [[sublane(cols[c], r) for c in range(r + 1)] for r in range(MICRO)]
        low = [[None] * MICRO for _ in range(MICRO)]
        rs = []
        for k in range(MICRO):
            r = lax.rsqrt(a[k][k])
            rs.append(r)
            for i in range(k + 1, MICRO):
                low[i][k] = a[i][k] * r
            for i in range(k + 1, MICRO):
                for c in range(k + 1, i + 1):
                    a[i][c] = a[i][c] - low[i][k] * low[c][k]
        us, vs = [], []
        for k in range(MICRO):
            u, v = sublane(d[g], k), sublane(e[g], k)
            for c in range(k):
                u = u - low[k][c] * us[c]
                v = v - low[k][c] * vs[c]
            us.append(u * rs[k])
            vs.append(v * rs[k])
        for h in range(g + 1, groups):
            ch = [lane(d[h], base + c) for c in range(MICRO)]
            ls = []
            for k in range(MICRO):
                t = ch[k]
                for c in range(k):
                    t = t - ls[c] * low[k][c]
                ls.append(t * rs[k])
            dh, eh = d[h], e[h]
            for k in range(MICRO):
                dh = dh - ls[k] * us[k]
                eh = eh - ls[k] * vs[k]
            d[h], e[h] = dh, eh
        sub = lax.broadcasted_iota(jnp.int32, (8, S), 0)
        for k in range(MICRO):
            d[g] = jnp.where(sub == k, us[k], d[g])
            e[g] = jnp.where(sub == k, vs[k], e[g])
    return d, e


def factor_tile(w, ti, base, hook, before_write):
    def part(b):
        return pl.ds(pl.multiple_of(base + b * S, S), S)

    sub = lax.broadcasted_iota(jnp.int32, (8, S), 0)
    lanes = lax.broadcasted_iota(jnp.int32, (8, S), 1)
    row = lax.broadcasted_iota(jnp.int32, (S, S), 0)
    col = lax.broadcasted_iota(jnp.int32, (S, S), 1)
    lower = row >= col
    t, inv = {}, {}
    for b in range(NB):
        hook(b)
        if b == 0:
            for i in range(NB):
                for j in range(i + 1):
                    x = w[part(i), part(j)]
                    t[i, j] = jnp.where(lower, x, x.T) if i == j else x
        x = t[b, b]
        eye = [(sub + 8 * g == lanes).astype(F32) for g in range(S // 8)]
        d, e = eliminate([x[8 * g : 8 * g + 8] for g in range(S // 8)], eye)
        if b == 0:
            before_write()
        upper = jnp.concatenate(d, 0)
        inverse = jnp.where(lower, jnp.concatenate(e, 0), 0.0)
        w[part(b), part(b)] = jnp.where(lower, upper.T, 0.0)
        inv[b, b] = inverse
        for i in range(b + 1, NB):
            t[i, b] = dot_nt(t[i, b], inverse, HIGHEST)
            w[part(i), part(b)] = t[i, b]
            w[part(b), part(i)] = jnp.zeros((S, S), F32)
        for i in range(b + 1, NB):
            for j in range(b + 1, i + 1):
                t[i, j] = t[i, j] - dot_nt(t[i, b], t[j, b], HIGHEST)
        for j in range(b):
            acc = None
            for k in range(j, b):
                term = dot_nn(t[b, k], inv[k, j], HIGHEST)
                acc = term if acc is None else acc + term
            inv[b, j] = -dot_nn(inverse, acc, HIGHEST)
        for j in range(NB):
            ti[b * S : (b + 1) * S, j * S : (j + 1) * S] = (
                inv[b, j] if j <= b else jnp.zeros((S, S), F32)
            )


def kernel(
    child, front, meta, panel_out, upd_out,
    recva, recvb, fr, total, half, w, ti, xs, st, recv2, meta_all, meta_s,
    s_meta, r_meta, s_a, r_a, s_b, r_b, s_fr, r_fr, s_p, r_p, s_sum, r_sum,
    s_hx, r_hx, s_ha, r_ha, s_hb, r_hb, s_st, r_st, lsem,
):
    me = lax.axis_index("row")
    col = lax.axis_index("col")
    y, z = me // 4, me % 4
    x, core = col // 2, col % 2
    first = jnp.where(core == 0, y, z)
    second = jnp.where(core == 0, z, y)
    my_chunk = second * 4 + first
    lead = x == 0

    def row_of(a, b):
        return jnp.where(core == 0, a * 4 + b, b * 4 + a)

    def peer(o):
        return (y + o // 4) % 4 * 4 + (z + o % 4) % 4

    def chunk_of(r):
        return jnp.where(core == 0, r % 4 * 4 + r // 4, r)

    def rows32(k):
        return pl.ds(pl.multiple_of(k * CHUNK, CHUNK), CHUNK)

    def remote(src, dst, send, recv, r, c):
        return pltpu.make_async_remote_copy(
            src, dst, send, recv, device_id=(r, c), device_id_type=MESH
        )

    barrier = pltpu.get_barrier_semaphore()

    def greet(r, c):
        pl.semaphore_signal(barrier, inc=1, device_id=(r, c), device_id_type=MESH)

    for o in ORDER:
        greet(peer(o), col)
    for t in range(1, 4):
        greet(me, (col + 2 * t) % 8)
        greet(row_of((first + t) % 4, second), x * 2 + 1 - core)
    greet(me, x * 2 + 1 - core)
    pl.semaphore_wait(barrier, 22)

    sibling = x * 2 + 1 - core

    def meta_copy(o):
        return remote(meta, meta_all.at[me], s_meta.at[o], r_meta.at[o], peer(o), col)

    def slots_a(o):
        r = peer(o)
        return remote(
            child.at[0:4, rows32(chunk_of(r)), :], recva.at[me], s_a.at[o], r_a.at[o], r, col
        )

    def slots_b(o):
        r = peer(o)
        return remote(
            child.at[4:8, rows32(chunk_of(r)), :], recvb.at[me], s_b.at[o], r_b.at[o], r, col
        )

    def front_copy(o):
        r = peer(o)
        return remote(front.at[chunk_of(r)], fr.at[me], s_fr.at[o], r_fr.at[o], r, col)

    def sum_copy(o):
        r = peer(o)
        return remote(total.at[r], recv2.at[my_chunk], s_sum.at[o], r_sum.at[o], r, col)

    for o in ORDER:
        meta_copy(o).start()

    @pl.when(lead & (y == 0))
    def _():
        for o in ORDER:
            front_copy(o).start()

    for o in ORDER:
        slots_a(o).start()
    own_a = pltpu.make_async_copy(child.at[0:4, rows32(my_chunk), :], recva.at[me], lsem.at[0])
    own_a.start()
    own_b = pltpu.make_async_copy(child.at[4:8, rows32(my_chunk), :], recvb.at[me], lsem.at[8])
    own_b.start()
    own_meta = pltpu.make_async_copy(meta, meta_all.at[me], lsem.at[1])
    own_meta.start()

    @pl.when(lead)
    def _():
        own = pltpu.make_async_copy(front.at[my_chunk], fr.at[me], lsem.at[2])
        own.start()
        own.wait()

    @pl.when(x > 0)
    def _():
        own = pltpu.make_async_copy(front, fr, lsem.at[3])
        own.start()
        own.wait()

    own_a.wait()
    own_b.wait()
    own_meta.wait()
    for o in ORDER:
        meta_copy(o).wait()
    to_smem = pltpu.make_async_copy(meta_all, meta_s, lsem.at[4])
    to_smem.start()
    to_smem.wait()
    for o in ORDER:
        slots_a(o).wait_recv()

    def reduce_for(d, late):
        def step(i, acc):
            slot = meta_s[i, 0, d]
            value = recva[i, jnp.minimum(slot, 3)]
            if late:
                value = jnp.where(slot < 4, value, recvb[i, jnp.maximum(slot - 4, 0)])
            code = meta_s[i, 1, d]
            left = jnp.where(code == 0, 1.0, 0.0)
            right = jnp.where(code == 1, 1.0, 0.0)
            return acc[0] + value * left, acc[1] + value * right

        zero = jnp.zeros((CHUNK, B), F32)
        a, b = lax.fori_loop(0, ROWS, step, (zero, zero))
        total[d, :, 0:B] = a
        total[d, :, B : 2 * B] = b

        @pl.when(lead)
        def _():
            total[d] = total[d] + fr[d]

    @pl.when(lead)
    def _():
        for t in range(4):
            o = y * 4 + t

            @pl.when(o > 0)
            def _():
                front_copy(o).wait_recv()

    for d in range(4):
        reduce_for(d, False)

    def piece_x(n, t):
        _, d, c0, nc = PIECES[n]
        part = w.at[pl.ds(pl.multiple_of(d * B + my_chunk * CHUNK, CHUNK), CHUNK), c0 : c0 + nc]
        return remote(part, part, s_p.at[n, t - 1], r_p.at[n, t - 1], me, (col + 2 * t) % 8)

    def piece_a(n, t):
        _, d, c0, nc = PIECES[n]
        part = w.at[pl.ds(pl.multiple_of(d * B + my_chunk * CHUNK, CHUNK), CHUNK), c0 : c0 + nc]
        return remote(
            part, part, s_p.at[n, 2 + t], r_p.at[n, 2 + t], row_of((first + t) % 4, second), col
        )

    def piece_b(n, t):
        _, d, c0, nc = PIECES[n]
        part = w.at[pl.ds(pl.multiple_of(d * B + second * S, S), S), c0 : c0 + nc]
        return remote(
            part, part, s_p.at[n, 5 + t], r_p.at[n, 5 + t], row_of(first, (second + t) % 4), col
        )

    def piece_s(n):
        _, d, c0, nc = PIECES[n]
        part = w.at[d * B : (d + 1) * B, c0 : c0 + nc]
        return remote(part, part, s_p.at[n, 9], r_p.at[n, 9], me, sibling)

    def on_core(k, numbers, action):
        @pl.when(core == k)
        def _():
            for n in numbers:
                if PIECES[n][0] == k:
                    action(n)

    def both_cores(numbers, action):
        for k in range(2):
            if any(PIECES[n][0] == k for n in numbers):
                on_core(k, numbers, action)

    def place(n):
        _, d, c0, nc = PIECES[n]
        lc = c0 % 1024
        w[pl.ds(pl.multiple_of(d * B + my_chunk * CHUNK, CHUNK), CHUNK), c0 : c0 + nc] = total[
            d, :, lc : lc + nc
        ]

    def start_x(n):
        for t in (1, 3, 2):
            piece_x(n, t).start()

    def wait_x(n):
        piece_x(n, x).wait_recv()

    def start_a(n):
        for t in (2, 1, 3):
            piece_a(n, t).start()

    def wait_a(n):
        for t in (1, 2, 3):
            piece_a(n, t).wait_recv()

    def start_b(n):
        for t in (2, 1, 3):
            piece_b(n, t).start()

    def wait_b(n):
        for t in (1, 2, 3):
            piece_b(n, t).wait_recv()

    def start_s(n):
        piece_s(n).start()

    def wait_s(n):
        piece_s(n).wait_recv()

    rest = tuple(range(1, len(PIECES)))

    @pl.when(lead)
    def _():
        both_cores((0,) + rest, place)
        both_cores((0,) + rest, start_x)

    @pl.when(x > 0)
    def _():
        both_cores((0,), wait_x)

    both_cores((0,), start_a)
    both_cores((0,), wait_a)
    both_cores((0,), start_b)

    @pl.when(x > 0)
    def _():
        both_cores(rest, wait_x)

    both_cores(rest, start_a)
    both_cores((0,), wait_b)
    both_cores((0,), start_s)
    for o in ORDER:
        slots_b(o).start()

    @pl.when(lead & (y > 0))
    def _():
        for o in ORDER:
            front_copy(o).start()

    @pl.when(core == 1)
    def _():
        wait_s(0)

    def half_x(t):
        to = (x + t) % 4
        return remote(
            total.at[pl.ds(to * 4, 4)], half.at[:, rows32(first), :],
            s_hx.at[t - 1], r_hx.at[t - 1], me, (col + 2 * t) % 8,
        )

    def half_a(t):
        part = half.at[:, rows32(first), :]
        return remote(part, part, s_ha.at[t - 1], r_ha.at[t - 1], row_of((first + t) % 4, second), col)

    def half_b(t, k, c):
        return remote(
            half.at[2 * k : 2 * k + 2],
            xs.at[:, pl.ds(pl.multiple_of(second * S, S), S), c * 1024 : (c + 1) * 1024],
            s_hb.at[t, k], r_hb.at[t, c], row_of(first, (second + t) % 4), x * 2 + k,
        )

    def strip_rows(n):
        return slice(n * 256, (n + 1) * 256)

    def strip_x(t, n, c):
        part = st.at[strip_rows(n), c * 1024 : (c + 1) * 1024]
        return remote(part, part, s_st.at[n, t], r_st.at[n, t], me, (col + 2 * t) % 8)

    def strip_s(c, k):
        part = st.at[:, c * 1024 : (c + 1) * 1024]
        return remote(part, part, s_st.at[0, 0], r_st.at[0, 0], me, sibling)

    def by_core(action):
        for c in range(2):

            @pl.when(core == c)
            def _():
                action(c)

    def task_rest_b():
        both_cores(rest, wait_a)
        both_cores(rest, start_b)

    def task_rest_s():
        both_cores(rest, wait_b)
        both_cores(rest, start_s)

    def task_sums():
        for o in ORDER:
            slots_b(o).wait_recv()

        @pl.when(lead)
        def _():
            for o in ORDER:

                @pl.when(y != o // 4)
                def _():
                    front_copy(o).wait_recv()

        lax.fori_loop(4, ROWS, lambda d, c: (reduce_for(d, True), c)[1], 0)

        @pl.when(lead)
        def _():
            for t in (1, 3, 2):
                half_x(t).start()

        for o in ORDER:
            sum_copy(o).start()
        recv2[my_chunk] = total[me]

    def task_half_a():
        @pl.when(x > 0)
        def _():
            half_x(x).wait_recv()
            for t in (2, 1, 3):
                half_a(t).start()

    def task_half_b():
        @pl.when(x > 0)
        def _():
            for t in (1, 2, 3):
                half_a(t).wait_recv()

            def send(c):
                for t in (2, 1, 3, 0):
                    for k in range(2):
                        if t > 0 or k != c:
                            half_b(t, k, c).start()
                own = pltpu.make_async_copy(
                    half.at[2 * c : 2 * c + 2],
                    xs.at[:, pl.ds(pl.multiple_of(second * S, S), S), c * 1024 : (c + 1) * 1024],
                    lsem.at[5],
                )
                own.start()
                own.wait()

            by_core(send)

    def task_assembled():
        for o in ORDER:
            sum_copy(o).wait_recv()

        @pl.when(x > 0)
        def _():
            recv2[...] = recv2[...] + fr[...]

        @pl.when(lead)
        def _():
            def put(c):
                def move(k, carry):
                    st[rows32(k), c * 1024 : (c + 1) * 1024] = recv2[k]
                    return carry

                lax.fori_loop(0, ROWS, move, 0)
                for n in range(2):
                    strip_x(1, n, c).start()
                    strip_x(3, 1 - n, c).start()
                strip_s(c, 1 - c).start()

            by_core(put)

    def task_forward():
        def forward(c):
            @pl.when(x == 1)
            def _():
                strip_x(1, 0, c).wait_recv()
                strip_x(1, 0, c).start()

            @pl.when(x == 3)
            def _():
                strip_x(3, 1, c).wait_recv()
                strip_x(3, 1, c).start()

        by_core(forward)

    def task_strip_s():
        def send(c):
            @pl.when(x == 1)
            def _():
                strip_x(1, 1, c).wait_recv()

            @pl.when(x == 3)
            def _():
                strip_x(3, 0, c).wait_recv()

            @pl.when(x == 2)
            def _():
                strip_x(1, 0, c).wait_recv()
                strip_x(3, 1, c).wait_recv()

            @pl.when(x > 0)
            def _():
                strip_s(c, 1 - c).start()

        by_core(send)

    schedule = {
        (0, 1): task_rest_b,
        (0, 2): task_rest_s,
        (2, 1): task_sums,
        (2, 3): task_half_a,
        (3, 1): task_half_b,
        (3, 0): task_assembled,
        (3, 3): task_forward,
    }

    def piece_done(n):
        @pl.when(lead)
        def _():
            for t in range(1, 4):
                piece_x(n, t).wait_send()

        for t in range(1, 4):
            piece_a(n, t).wait_send()
            piece_b(n, t).wait_send()
        piece_s(n).wait_send()

    def tile(p, carry):
        base = pl.multiple_of(p * B, B)

        def hook(b):
            for (p0, b0), task in schedule.items():
                if b0 == b:
                    pl.when(p == p0)(task)

        def before_write():
            pl.when(p == 0)(lambda: both_cores((0,), piece_done))

        factor_tile(w, ti.at[p], base, hook, before_write)

        @pl.when(p == 0)
        def _():
            @pl.when(core == 0)
            def _():
                for n in rest:
                    if PIECES[n][0] == 1:
                        wait_s(n)

            @pl.when(core == 1)
            def _():
                for n in rest:
                    if PIECES[n][0] == 0:
                        wait_s(n)

            both_cores(rest, piece_done)

        here = pl.ds(base, B)

        def solve(q, c):
            o = pl.ds(pl.multiple_of(q * B, B), B)
            w[o, here] = dot_nt(w[o, here], ti[p], HIGH)
            return c

        lax.fori_loop(p + 1, NP, solve, 0)

        def update(q, c):
            o = pl.ds(pl.multiple_of(q * B, B), B)
            w[here, o] = jnp.zeros((B, B), F32)

            def inner(s, c):
                o2 = pl.ds(pl.multiple_of(s * B, B), B)
                w[o, o2] = w[o, o2] - dot_nt(w[o, here], w[o2, here], HIGH)
                return c

            return lax.fori_loop(p + 1, q + 1, inner, c)

        lax.fori_loop(p + 1, NP, update, 0)
        return carry

    lax.fori_loop(0, NP, tile, 0)
    task_strip_s()

    def solve_rows(ref):
        def panel(p, c):
            here = pl.ds(pl.multiple_of(p * B, B), B)
            ref[:, here] = dot_nt(ref[:, here], ti[p], HIGH)

            def later(q, c):
                o = pl.ds(pl.multiple_of(q * B, B), B)
                ref[:, o] = ref[:, o] - dot_nt(ref[:, here], w[o, here], HIGH)
                return c

            return lax.fori_loop(p + 1, NP, later, c)

        lax.fori_loop(0, NP, panel, 0)

    @pl.when(lead)
    def _():
        for k in range(2):
            xs[k] = w[pl.ds(pl.multiple_of((2 * core + k) * B, B), B), :]

    @pl.when(x > 0)
    def _():
        for t in range(1, 4):
            for c in range(2):
                half_b(t, 0, c).wait_recv()

        def others(c):
            half_b(0, 0, 1 - c).wait_recv()

        by_core(others)
        for k in range(2):
            solve_rows(xs.at[k])

    def strip_done(c):
        strip_s(c, 1 - c).wait()

        @pl.when(lead)
        def _():
            for n in range(2):
                strip_x(1, n, c).wait_send()
                strip_x(3, n, c).wait_send()

        @pl.when(x == 1)
        def _():
            strip_x(1, 0, c).wait_send()

        @pl.when(x == 3)
        def _():
            strip_x(3, 1, c).wait_send()

    by_core(strip_done)

    @pl.when(y == 0)
    def _():
        st[...] = w[pl.ds(pl.multiple_of(me * B, B), B), :]

    @pl.when(y > 0)
    def _():
        solve_rows(st)

    panel_copy = pltpu.make_async_copy(st, panel_out, lsem.at[6])
    panel_copy.start()

    def last(i, c):
        rows = pl.ds(pl.multiple_of(i * 256, 256), 256)
        for k in range(2):
            product = dot_nt(st[rows, :], xs[k], HIGH)
            part = recv2[pl.ds(i * 8, 8), :, k * B : (k + 1) * B]
            recv2[pl.ds(i * 8, 8), :, k * B : (k + 1) * B] = part - product.reshape(8, CHUNK, B)
        return c

    lax.fori_loop(0, 2, last, 0)
    out_copy = pltpu.make_async_copy(recv2, upd_out, lsem.at[7])
    out_copy.start()

    for o in ORDER:
        slots_a(o).wait_send()
        slots_b(o).wait_send()
        sum_copy(o).wait_send()

    @pl.when(lead)
    def _():
        for o in ORDER:
            front_copy(o).wait_send()
        for t in range(1, 4):
            half_x(t).wait_send()


    @pl.when(x > 0)
    def _():
        for t in range(1, 4):
            half_a(t).wait_send()

        def half_sent(c):
            for t in range(4):
                for k in range(2):
                    if t > 0 or k != c:
                        half_b(t, k, c).wait_send()

        by_core(half_sent)

    panel_copy.wait()
    out_copy.wait()


def fused(front, child, meta):
    dma = pltpu.SemaphoreType.DMA
    return pl.pallas_call(
        kernel,
        out_shape=[
            jax.ShapeDtypeStruct((B, NP * B), F32),
            jax.ShapeDtypeStruct((ROWS, CHUNK, 1024), F32),
        ],
        in_specs=[
            pl.BlockSpec(memory_space=pl.ANY),
            pl.BlockSpec(memory_space=pl.ANY),
            pl.BlockSpec(memory_space=pltpu.VMEM),
        ],
        out_specs=[pl.BlockSpec(memory_space=pl.ANY)] * 2,
        scratch_shapes=[
            pltpu.VMEM((ROWS, 4, CHUNK, B), F32),
            pltpu.VMEM((ROWS, 4, CHUNK, B), F32),
            pltpu.VMEM((ROWS, CHUNK, 1024), F32),
            pltpu.VMEM((ROWS, CHUNK, 1024), F32),
            pltpu.VMEM((4, S, 1024), F32),
            pltpu.VMEM((NP * B, NP * B), F32),
            pltpu.VMEM((NP, B, B), F32),
            pltpu.VMEM((2, B, NP * B), F32),
            pltpu.VMEM((B, NP * B), F32),
            pltpu.VMEM((ROWS, CHUNK, 1024), F32),
            pltpu.VMEM((ROWS, 8, 128), jnp.int32),
            pltpu.SMEM((ROWS, 8, 128), jnp.int32),
            dma((16,)), dma((16,)), dma((16,)), dma((16,)), dma((16,)), dma((16,)),
            dma((16,)), dma((16,)), dma((6, 10)), dma((6, 10)), dma((16,)), dma((16,)),
            dma((3,)), dma((3,)), dma((3,)), dma((3,)), dma((4, 2)), dma((4, 2)),
            dma((2, 4)), dma((2, 4)), dma((9,)),
        ],
        compiler_params=pltpu.CompilerParams(
            collective_id=0, has_side_effects=True, vmem_limit_bytes=60 * 2**20
        ),
    )(child, front, meta)


def tables(child_target, child_count):
    targets = child_target.reshape(CT, 2)
    slots = jnp.arange(CT, dtype=jnp.int32)
    live = slots < child_count.reshape(())
    key = jnp.where(live, targets[:, 0], ROWS) * CT + slots
    place = jnp.sum((key[None, :] < key[:, None]).astype(jnp.int32), axis=1)
    order = jnp.sum(jnp.where(place[:, None] == slots[None, :], slots[:, None], 0), axis=0)
    hit = (targets[:, 0][:, None] == jnp.arange(ROWS)[None, :]) & live[:, None]
    where = jnp.sum(jnp.where(hit, place[:, None], 0), axis=0)
    code = jnp.sum(jnp.where(hit, targets[:, 1][:, None] % 2, 0), axis=0)
    code = jnp.where(hit.any(axis=0), code, 2)
    table = jnp.stack([where, code]).astype(jnp.int32)
    return order.astype(jnp.int32), jnp.pad(table, ((0, 6), (0, 128 - ROWS)))


def sort_kernel(order, child, out, held, sems):
    reads = [pltpu.make_async_copy(child.at[order[i]], held.at[i], sems.at[i]) for i in range(CT)]
    writes = [pltpu.make_async_copy(held.at[i], out.at[i], sems.at[CT + i]) for i in range(CT)]
    for copy in reads:
        copy.start()
    for i in range(CT):
        reads[i].wait()
        writes[i].start()
    for copy in writes:
        copy.wait()


def sort_slots(order, child):
    return pl.pallas_call(
        sort_kernel,
        out_shape=jax.ShapeDtypeStruct(child.shape, F32),
        in_specs=[pl.BlockSpec(memory_space=pltpu.SMEM), pl.BlockSpec(memory_space=pl.ANY)],
        out_specs=pl.BlockSpec(memory_space=pl.ANY),
        scratch_shapes=[pltpu.VMEM((CT, B, B), F32), pltpu.SemaphoreType.DMA((2 * CT,))],
        compiler_params=pltpu.CompilerParams(vmem_limit_bytes=32 * 2**20),
    )(order, child)


def body(front, child_tiles, child_target, child_count):
    order, meta = tables(child_target, child_count)
    child = sort_slots(order, child_tiles.reshape(CT, B, B))
    panel, updated = fused(front.reshape(ROWS, CHUNK, 1024), child, meta)
    return panel, updated.reshape(front.shape)


def solution(mesh):
    return jax.shard_map(
        body,
        mesh=mesh,
        in_specs=(
            P("row", "col"),
            P("row", "col", None, None),
            P("row", "col", None),
            P("row", "col"),
        ),
        out_specs=(P("row", None), P("row", "col")),
        check_vma=False,
    )
```

```python
import jax
import jax.numpy as jnp
from jax import lax
from jax.experimental import pallas as pl
from jax.experimental.pallas import tpu as pltpu
from jax.sharding import PartitionSpec as P

MESH = pl.DeviceIdType.MESH
F32 = jnp.float32
HIGHEST = lax.Precision.HIGHEST
HIGH = lax.Precision.HIGH
ROWS = 16
CT = 8
B = 512
S = 128
NP = 4
CHUNK = 32
MICRO = 8
NB = B // S
ORDER = (10, 9, 11, 6, 14, 5, 7, 13, 15, 2, 8, 1, 3, 4, 12)
PIECES = (
    (0, 0, 0, 512),
    (0, 1, 0, 1024),
    (0, 2, 0, 1024),
    (0, 3, 0, 1024),
    (1, 2, 1024, 512),
    (1, 3, 1024, 1024),
)


def dot_nt(a, b, precision):
    return lax.dot_general(
        a, b, (((1,), (1,)), ((), ())), precision=precision, preferred_element_type=F32
    )


def dot_nn(a, b, precision):
    return lax.dot_general(
        a, b, (((1,), (0,)), ((), ())), precision=precision, preferred_element_type=F32
    )


def lane(x, j):
    return jnp.broadcast_to(x[:, j : j + 1], x.shape)


def sublane(x, s):
    return jnp.broadcast_to(x[s : s + 1, :], x.shape)


def eliminate(d, e):
    groups = len(d)
    for g in range(groups):
        base = MICRO * g
        cols = [lane(d[g], base + c) for c in range(MICRO)]
        a = [[sublane(cols[c], r) for c in range(r + 1)] for r in range(MICRO)]
        low = [[None] * MICRO for _ in range(MICRO)]
        rs = []
        for k in range(MICRO):
            r = lax.rsqrt(a[k][k])
            rs.append(r)
            for i in range(k + 1, MICRO):
                low[i][k] = a[i][k] * r
            for i in range(k + 1, MICRO):
                for c in range(k + 1, i + 1):
                    a[i][c] = a[i][c] - low[i][k] * low[c][k]
        us, vs = [], []
        for k in range(MICRO):
            u, v = sublane(d[g], k), sublane(e[g], k)
            for c in range(k):
                u = u - low[k][c] * us[c]
                v = v - low[k][c] * vs[c]
            us.append(u * rs[k])
            vs.append(v * rs[k])
        for h in range(g + 1, groups):
            ch = [lane(d[h], base + c) for c in range(MICRO)]
            ls = []
            for k in range(MICRO):
                t = ch[k]
                for c in range(k):
                    t = t - ls[c] * low[k][c]
                ls.append(t * rs[k])
            dh, eh = d[h], e[h]
            for k in range(MICRO):
                dh = dh - ls[k] * us[k]
                eh = eh - ls[k] * vs[k]
            d[h], e[h] = dh, eh
        sub = lax.broadcasted_iota(jnp.int32, (8, S), 0)
        for k in range(MICRO):
            d[g] = jnp.where(sub == k, us[k], d[g])
            e[g] = jnp.where(sub == k, vs[k], e[g])
    return d, e


def factor_tile(w, ti, base, hook, before_write):
    def part(b):
        return pl.ds(pl.multiple_of(base + b * S, S), S)

    sub = lax.broadcasted_iota(jnp.int32, (8, S), 0)
    lanes = lax.broadcasted_iota(jnp.int32, (8, S), 1)
    row = lax.broadcasted_iota(jnp.int32, (S, S), 0)
    col = lax.broadcasted_iota(jnp.int32, (S, S), 1)
    lower = row >= col
    t, inv = {}, {}
    for b in range(NB):
        hook(b)
        if b == 0:
            for i in range(NB):
                for j in range(i + 1):
                    x = w[part(i), part(j)]
                    t[i, j] = jnp.where(lower, x, x.T) if i == j else x
        x = t[b, b]
        eye = [(sub + 8 * g == lanes).astype(F32) for g in range(S // 8)]
        d, e = eliminate([x[8 * g : 8 * g + 8] for g in range(S // 8)], eye)
        if b == 0:
            before_write()
        upper = jnp.concatenate(d, 0)
        inverse = jnp.where(lower, jnp.concatenate(e, 0), 0.0)
        w[part(b), part(b)] = jnp.where(lower, upper.T, 0.0)
        inv[b, b] = inverse
        for i in range(b + 1, NB):
            t[i, b] = dot_nt(t[i, b], inverse, HIGHEST)
            w[part(i), part(b)] = t[i, b]
            w[part(b), part(i)] = jnp.zeros((S, S), F32)
        for i in range(b + 1, NB):
            for j in range(b + 1, i + 1):
                t[i, j] = t[i, j] - dot_nt(t[i, b], t[j, b], HIGHEST)
        for j in range(b):
            acc = None
            for k in range(j, b):
                term = dot_nn(t[b, k], inv[k, j], HIGHEST)
                acc = term if acc is None else acc + term
            inv[b, j] = -dot_nn(inverse, acc, HIGHEST)
        for j in range(NB):
            ti[b * S : (b + 1) * S, j * S : (j + 1) * S] = (
                inv[b, j] if j <= b else jnp.zeros((S, S), F32)
            )


def kernel(
    child, front, meta, panel_out, upd_out,
    recva, recvb, fr, own_front, total, half, w, ti, xs, st, recv2, meta_all, meta_s,
    s_meta, r_meta, s_a, r_a, s_b, r_b, s_fr, r_fr, s_p, r_p, s_sum, r_sum,
    s_hx, r_hx, s_ha, r_ha, s_hb, r_hb, s_st, r_st, lsem,
):
    me = lax.axis_index("row")
    col = lax.axis_index("col")
    y, z = me // 4, me % 4
    x, core = col // 2, col % 2
    first = jnp.where(core == 0, y, z)
    second = jnp.where(core == 0, z, y)
    my_chunk = second * 4 + first
    lead = x == 0

    def row_of(a, b):
        return jnp.where(core == 0, a * 4 + b, b * 4 + a)

    def peer(o):
        return (y + o // 4) % 4 * 4 + (z + o % 4) % 4

    def chunk_of(r):
        return jnp.where(core == 0, r % 4 * 4 + r // 4, r)

    def rows32(k):
        return pl.ds(pl.multiple_of(k * CHUNK, CHUNK), CHUNK)

    def remote(src, dst, send, recv, r, c):
        return pltpu.make_async_remote_copy(
            src, dst, send, recv, device_id=(r, c), device_id_type=MESH
        )

    barrier = pltpu.get_barrier_semaphore()

    def greet(r, c):
        pl.semaphore_signal(barrier, inc=1, device_id=(r, c), device_id_type=MESH)

    for o in ORDER:
        greet(peer(o), col)
    for t in range(1, 4):
        greet(me, (col + 2 * t) % 8)
        greet(row_of((first + t) % 4, second), x * 2 + 1 - core)
    greet(me, x * 2 + 1 - core)

    @pl.when(x > 0)
    def _():
        for d in range(4):
            greet(x * 4 + d, core)

    pl.semaphore_wait(barrier, 22 + jnp.where(lead & (y > 0), ROWS, 0))

    sibling = x * 2 + 1 - core

    def meta_copy(o):
        return remote(meta, meta_all.at[me], s_meta.at[o], r_meta.at[o], peer(o), col)

    def slots_a(o):
        r = peer(o)
        return remote(
            child.at[0:4, rows32(chunk_of(r)), :], recva.at[me], s_a.at[o], r_a.at[o], r, col
        )

    def slots_b(o):
        r = peer(o)
        return remote(
            child.at[4:8, rows32(chunk_of(r)), :], recvb.at[me], s_b.at[o], r_b.at[o], r, col
        )

    def front_copy(r):
        return remote(front.at[chunk_of(r)], fr.at[z], s_fr.at[r], r_fr.at[z], r, y * 2 + core)

    def front_from(d):
        return remote(front.at[0], fr.at[d], s_fr.at[0], r_fr.at[d], me, y * 2 + core)

    def sum_copy(o):
        r = peer(o)
        return remote(total.at[r], recv2.at[my_chunk], s_sum.at[o], r_sum.at[o], r, col)

    for o in ORDER:
        meta_copy(o).start()

    def send_front():
        def send(r, carry):
            pl.when((r != me) | (y > 0))(lambda: front_copy(r).start())
            return carry

        lax.fori_loop(0, ROWS, send, 0)

    front_first = lead & (me == 0) & (core == 0)
    front_next = lead & (y == 0) & ((core == 0) & (z > 0) | (z > 1))
    front_late = lead & (y > 0)
    pl.when(front_first)(send_front)
    for o in ORDER:
        slots_a(o).start()
    pl.when(front_next)(send_front)
    own_a = pltpu.make_async_copy(child.at[0:4, rows32(my_chunk), :], recva.at[me], lsem.at[0])
    own_a.start()
    own_b = pltpu.make_async_copy(child.at[4:8, rows32(my_chunk), :], recvb.at[me], lsem.at[8])
    own_b.start()
    own_meta = pltpu.make_async_copy(meta, meta_all.at[me], lsem.at[1])
    own_meta.start()

    keep_front = pltpu.make_async_copy(front, own_front, lsem.at[3])
    keep_front.start()

    @pl.when(lead & (y == 0))
    def _():
        own = pltpu.make_async_copy(front.at[my_chunk], fr.at[z], lsem.at[2])
        own.start()
        own.wait()

    own_a.wait()
    own_b.wait()
    own_meta.wait()
    for o in ORDER:
        meta_copy(o).wait()
    to_smem = pltpu.make_async_copy(meta_all, meta_s, lsem.at[4])
    to_smem.start()
    to_smem.wait()
    for o in ORDER:
        slots_a(o).wait_recv()

    def reduce_for(d, late):
        def step(i, acc):
            slot = meta_s[i, 0, d]
            value = recva[i, jnp.minimum(slot, 3)]
            if late:
                value = jnp.where(slot < 4, value, recvb[i, jnp.maximum(slot - 4, 0)])
            code = meta_s[i, 1, d]
            left = jnp.where(code == 0, 1.0, 0.0)
            right = jnp.where(code == 1, 1.0, 0.0)
            return acc[0] + value * left, acc[1] + value * right

        zero = jnp.zeros((CHUNK, B), F32)
        a, b = lax.fori_loop(0, ROWS, step, (zero, zero))
        total[d, :, 0:B] = a
        total[d, :, B : 2 * B] = b

    def wait_front(numbers):
        for d in numbers:
            pl.when((x > 0) | (y > 0) | (z != d))(lambda d=d: front_from(d).wait_recv())

    reduce_for(0, False)

    def piece_x(n, t):
        _, d, c0, nc = PIECES[n]
        part = w.at[pl.ds(pl.multiple_of(d * B + my_chunk * CHUNK, CHUNK), CHUNK), c0 : c0 + nc]
        return remote(part, part, s_p.at[n, t - 1], r_p.at[n, t - 1], me, (col + 2 * t) % 8)

    def piece_a(n, t):
        _, d, c0, nc = PIECES[n]
        part = w.at[pl.ds(pl.multiple_of(d * B + my_chunk * CHUNK, CHUNK), CHUNK), c0 : c0 + nc]
        return remote(
            part, part, s_p.at[n, 2 + t], r_p.at[n, 2 + t], row_of((first + t) % 4, second), col
        )

    def piece_b(n, t):
        _, d, c0, nc = PIECES[n]
        part = w.at[pl.ds(pl.multiple_of(d * B + second * S, S), S), c0 : c0 + nc]
        return remote(
            part, part, s_p.at[n, 5 + t], r_p.at[n, 5 + t], row_of(first, (second + t) % 4), col
        )

    def piece_s(n):
        _, d, c0, nc = PIECES[n]
        part = w.at[d * B : (d + 1) * B, c0 : c0 + nc]
        return remote(part, part, s_p.at[n, 9], r_p.at[n, 9], me, sibling)

    def on_core(k, numbers, action):
        @pl.when(core == k)
        def _():
            for n in numbers:
                if PIECES[n][0] == k:
                    action(n)

    def both_cores(numbers, action):
        for k in range(2):
            if any(PIECES[n][0] == k for n in numbers):
                on_core(k, numbers, action)

    def place(n):
        _, d, c0, nc = PIECES[n]
        lc = c0 % 1024
        w[pl.ds(pl.multiple_of(d * B + my_chunk * CHUNK, CHUNK), CHUNK), c0 : c0 + nc] = (
            total[d, :, lc : lc + nc] + fr[d, :, lc : lc + nc]
        )

    def start_x(n):
        for t in (1, 3, 2):
            piece_x(n, t).start()

    def wait_x(n):
        piece_x(n, x).wait_recv()

    def start_a(n):
        for t in (2, 1, 3):
            piece_a(n, t).start()

    def wait_a(n):
        for t in (1, 2, 3):
            piece_a(n, t).wait_recv()

    def start_b(n):
        for t in (2, 1, 3):
            piece_b(n, t).start()

    def wait_b(n):
        for t in (1, 2, 3):
            piece_b(n, t).wait_recv()

    def start_s(n):
        piece_s(n).start()

    def wait_s(n):
        piece_s(n).wait_recv()

    rest = tuple(range(1, len(PIECES)))

    @pl.when(lead & (core == 0))
    def _():
        wait_front((0,))
        place(0)
        start_x(0)

    for d in range(1, 4):
        reduce_for(d, False)

    @pl.when(x > 0)
    def _():
        both_cores((0,), wait_x)

    both_cores((0,), start_a)

    @pl.when(lead)
    def _():
        pl.when(core == 0)(lambda: wait_front((1, 2, 3)))
        pl.when(core == 1)(lambda: wait_front((2, 3)))
        both_cores(rest, place)
        both_cores(rest, start_x)

    both_cores((0,), wait_a)
    both_cores((0,), start_b)
    pl.when(front_late)(send_front)

    @pl.when(x > 0)
    def _():
        both_cores(rest, wait_x)

    both_cores(rest, start_a)
    both_cores((0,), wait_b)
    both_cores((0,), start_s)
    for o in ORDER:
        slots_b(o).start()

    @pl.when(core == 1)
    def _():
        wait_s(0)

    def half_x(t):
        to = (x + t) % 4
        return remote(
            total.at[pl.ds(to * 4, 4)], half.at[:, rows32(first), :],
            s_hx.at[t - 1], r_hx.at[t - 1], me, (col + 2 * t) % 8,
        )

    def half_a(t):
        part = half.at[:, rows32(first), :]
        return remote(part, part, s_ha.at[t - 1], r_ha.at[t - 1], row_of((first + t) % 4, second), col)

    def half_b(t, k, c):
        return remote(
            half.at[2 * k : 2 * k + 2],
            xs.at[:, pl.ds(pl.multiple_of(second * S, S), S), c * 1024 : (c + 1) * 1024],
            s_hb.at[t, k], r_hb.at[t, c], row_of(first, (second + t) % 4), x * 2 + k,
        )

    def strip_x(n, c):
        part = st.at[n * 64 : (n + 1) * 64, c * 1024 : (c + 1) * 1024]
        t = 1 if n < 4 else 3
        return remote(part, part, s_st.at[0, n], r_st.at[0, n], me, (col + 2 * t) % 8)

    def strip_s(n, c):
        part = st.at[n * 64 : (n + 1) * 64, c * 1024 : (c + 1) * 1024]
        return remote(part, part, s_st.at[1, n], r_st.at[1, n], me, sibling)

    def by_core(action):
        for c in range(2):

            @pl.when(core == c)
            def _():
                action(c)

    def task_rest_b():
        both_cores(rest, wait_a)
        both_cores(rest, start_b)

    def task_rest_s():
        both_cores(rest, wait_b)
        both_cores(rest, start_s)

    def task_sums():
        for o in ORDER:
            slots_b(o).wait_recv()

        lax.fori_loop(4, ROWS, lambda d, c: (reduce_for(d, True), c)[1], 0)

        @pl.when(lead)
        def _():
            for t in (1, 3, 2):
                half_x(t).start()
            for o in ORDER:
                sum_copy(o).start()

        recv2[my_chunk] = total[me]

    def task_half_a():
        @pl.when(x > 0)
        def _():
            half_x(x).wait_recv()
            wait_front(range(4))
            half[:, rows32(first), :] = half[:, rows32(first), :] + fr[...]
            for t in (2, 1, 3):
                half_a(t).start()

    def task_half_b():
        @pl.when(x > 0)
        def _():
            for t in (1, 2, 3):
                half_a(t).wait_recv()

            def send(c):
                for t in (2, 1, 3, 0):
                    for k in range(2):
                        if t > 0 or k != c:
                            half_b(t, k, c).start()
                own = pltpu.make_async_copy(
                    half.at[2 * c : 2 * c + 2],
                    xs.at[:, pl.ds(pl.multiple_of(second * S, S), S), c * 1024 : (c + 1) * 1024],
                    lsem.at[5],
                )
                own.start()
                own.wait()

            by_core(send)
            for o in ORDER:
                sum_copy(o).start()

    def assemble():
        for o in ORDER:
            sum_copy(o).wait_recv()
        keep_front.wait()
        recv2[...] = recv2[...] + own_front[...]

    def task_assembled():
        @pl.when(lead)
        def _():
            assemble()

            def put(c):
                def move(k, carry):
                    st[rows32(k), c * 1024 : (c + 1) * 1024] = recv2[k]
                    return carry

                lax.fori_loop(0, ROWS, move, 0)
                for n in range(4):
                    strip_x(n, c).start()
                    strip_x(n + 4, c).start()
                for n in range(8):
                    strip_s(n, c).start()

            by_core(put)

    def pass_on(n, c):
        strip_x(n, c).wait_recv()
        pl.when((x < 3) if n < 4 else (x > 1))(lambda: strip_x(n, c).start())
        strip_s(n, c).start()

    def task_forward(stages):
        def forward(k, c):
            for stage in stages:
                for n, later in ((stage - k + 1, k - 1), (stage - 3 + k + 4, 3 - k)):
                    if 0 <= stage - later < 4:
                        pass_on(n, c)

        for k in range(1, 4):
            for c in range(2):
                pl.when((x == k) & (core == c))(lambda k=k, c=c: forward(k, c))

    schedule = {
        (0, 1): task_rest_b,
        (0, 2): task_rest_s,
        (2, 0): task_sums,
        (2, 2): task_half_a,
        (2, 3): task_assembled,
        (3, 0): task_half_b,
        (3, 1): lambda: task_forward((0, 1)),
        (3, 2): lambda: task_forward((2, 3)),
        (3, 3): lambda: task_forward((4, 5)),
    }

    def piece_done(n):
        @pl.when(lead)
        def _():
            for t in range(1, 4):
                piece_x(n, t).wait_send()

        for t in range(1, 4):
            piece_a(n, t).wait_send()
            piece_b(n, t).wait_send()
        piece_s(n).wait_send()

    def tile(p, carry):
        base = pl.multiple_of(p * B, B)

        def hook(b):
            for (p0, b0), task in schedule.items():
                if b0 == b:
                    pl.when(p == p0)(task)

        def before_write():
            pl.when(p == 0)(lambda: both_cores((0,), piece_done))

        factor_tile(w, ti.at[p], base, hook, before_write)

        @pl.when(p == 0)
        def _():
            @pl.when(core == 0)
            def _():
                for n in rest:
                    if PIECES[n][0] == 1:
                        wait_s(n)

            @pl.when(core == 1)
            def _():
                for n in rest:
                    if PIECES[n][0] == 0:
                        wait_s(n)

            both_cores(rest, piece_done)

        here = pl.ds(base, B)

        def solve(q, c):
            o = pl.ds(pl.multiple_of(q * B, B), B)
            w[o, here] = dot_nt(w[o, here], ti[p], HIGH)
            return c

        lax.fori_loop(p + 1, NP, solve, 0)

        def update(q, c):
            o = pl.ds(pl.multiple_of(q * B, B), B)
            w[here, o] = jnp.zeros((B, B), F32)

            def inner(s, c):
                o2 = pl.ds(pl.multiple_of(s * B, B), B)
                w[o, o2] = w[o, o2] - dot_nt(w[o, here], w[o2, here], HIGH)
                return c

            return lax.fori_loop(p + 1, q + 1, inner, c)

        lax.fori_loop(p + 1, NP, update, 0)
        return carry

    lax.fori_loop(0, NP, tile, 0)

    def solve_rows(ref):
        def panel(p, c):
            here = pl.ds(pl.multiple_of(p * B, B), B)
            ref[:, here] = dot_nt(ref[:, here], ti[p], HIGH)

            def later(q, c):
                o = pl.ds(pl.multiple_of(q * B, B), B)
                ref[:, o] = ref[:, o] - dot_nt(ref[:, here], w[o, here], HIGH)
                return c

            return lax.fori_loop(p + 1, NP, later, c)

        lax.fori_loop(0, NP, panel, 0)

    @pl.when(lead)
    def _():
        for k in range(2):
            xs[k] = w[pl.ds(pl.multiple_of((2 * core + k) * B, B), B), :]

    @pl.when(x > 0)
    def _():
        for t in range(1, 4):
            for c in range(2):
                half_b(t, 0, c).wait_recv()

        def others(c):
            half_b(0, 0, 1 - c).wait_recv()

        by_core(others)
        for k in range(2):
            solve_rows(xs.at[k])

    def strip_done(c):
        for n in range(8):
            strip_s(n, c).wait()
        for n in range(4):
            pl.when(x < 3)(lambda: strip_x(n, c).wait_send())
            pl.when((x == 0) | (x > 1))(lambda: strip_x(n + 4, c).wait_send())

    by_core(strip_done)

    @pl.when(y == 0)
    def _():
        st[...] = w[pl.ds(pl.multiple_of(me * B, B), B), :]

    @pl.when(y > 0)
    def _():
        solve_rows(st)

    panel_copy = pltpu.make_async_copy(st, panel_out, lsem.at[6])
    panel_copy.start()
    pl.when(x > 0)(assemble)

    def last(i, c):
        rows = pl.ds(pl.multiple_of(i * 256, 256), 256)
        for k in range(2):
            product = dot_nt(st[rows, :], xs[k], HIGH)
            part = recv2[pl.ds(i * 8, 8), :, k * B : (k + 1) * B]
            recv2[pl.ds(i * 8, 8), :, k * B : (k + 1) * B] = part - product.reshape(8, CHUNK, B)
        return c

    lax.fori_loop(0, 2, last, 0)
    out_copy = pltpu.make_async_copy(recv2, upd_out, lsem.at[7])
    out_copy.start()

    for o in ORDER:
        slots_a(o).wait_send()
        slots_b(o).wait_send()
        sum_copy(o).wait_send()

    @pl.when(front_first | front_next | front_late)
    def _():
        def sent(r, carry):
            pl.when((r != me) | (y > 0))(lambda: front_copy(r).wait_send())
            return carry

        lax.fori_loop(0, ROWS, sent, 0)

    @pl.when(lead)
    def _():
        for t in range(1, 4):
            half_x(t).wait_send()


    @pl.when(x > 0)
    def _():
        for t in range(1, 4):
            half_a(t).wait_send()

        def half_sent(c):
            for t in range(4):
                for k in range(2):
                    if t > 0 or k != c:
                        half_b(t, k, c).wait_send()

        by_core(half_sent)

    panel_copy.wait()
    out_copy.wait()


def fused(front, child, meta):
    dma = pltpu.SemaphoreType.DMA
    return pl.pallas_call(
        kernel,
        out_shape=[
            jax.ShapeDtypeStruct((B, NP * B), F32),
            jax.ShapeDtypeStruct((ROWS, CHUNK, 1024), F32),
        ],
        in_specs=[
            pl.BlockSpec(memory_space=pl.ANY),
            pl.BlockSpec(memory_space=pl.ANY),
            pl.BlockSpec(memory_space=pltpu.VMEM),
        ],
        out_specs=[pl.BlockSpec(memory_space=pl.ANY)] * 2,
        scratch_shapes=[
            pltpu.VMEM((ROWS, 4, CHUNK, B), F32),
            pltpu.VMEM((ROWS, 4, CHUNK, B), F32),
            pltpu.VMEM((4, CHUNK, 1024), F32),
            pltpu.VMEM((ROWS, CHUNK, 1024), F32),
            pltpu.VMEM((ROWS, CHUNK, 1024), F32),
            pltpu.VMEM((4, S, 1024), F32),
            pltpu.VMEM((NP * B, NP * B), F32),
            pltpu.VMEM((NP, B, B), F32),
            pltpu.VMEM((2, B, NP * B), F32),
            pltpu.VMEM((B, NP * B), F32),
            pltpu.VMEM((ROWS, CHUNK, 1024), F32),
            pltpu.VMEM((ROWS, 8, 128), jnp.int32),
            pltpu.SMEM((ROWS, 8, 128), jnp.int32),
            dma((16,)), dma((16,)), dma((16,)), dma((16,)), dma((16,)), dma((16,)),
            dma((16,)), dma((16,)), dma((6, 10)), dma((6, 10)), dma((16,)), dma((16,)),
            dma((3,)), dma((3,)), dma((3,)), dma((3,)), dma((4, 2)), dma((4, 2)),
            dma((2, 8)), dma((2, 8)), dma((9,)),
        ],
        compiler_params=pltpu.CompilerParams(
            collective_id=0, has_side_effects=True, vmem_limit_bytes=60 * 2**20
        ),
    )(child, front, meta)


def tables(child_target, child_count):
    targets = child_target.reshape(CT, 2)
    slots = jnp.arange(CT, dtype=jnp.int32)
    live = slots < child_count.reshape(())
    key = jnp.where(live, targets[:, 0], ROWS) * CT + slots
    place = jnp.sum((key[None, :] < key[:, None]).astype(jnp.int32), axis=1)
    order = jnp.sum(jnp.where(place[:, None] == slots[None, :], slots[:, None], 0), axis=0)
    hit = (targets[:, 0][:, None] == jnp.arange(ROWS)[None, :]) & live[:, None]
    where = jnp.sum(jnp.where(hit, place[:, None], 0), axis=0)
    code = jnp.sum(jnp.where(hit, targets[:, 1][:, None] % 2, 0), axis=0)
    code = jnp.where(hit.any(axis=0), code, 2)
    table = jnp.stack([where, code]).astype(jnp.int32)
    return order.astype(jnp.int32), jnp.pad(table, ((0, 6), (0, 128 - ROWS)))


def sort_kernel(order, child, out, held, sems):
    reads = [pltpu.make_async_copy(child.at[order[i]], held.at[i], sems.at[i]) for i in range(CT)]
    writes = [pltpu.make_async_copy(held.at[i], out.at[i], sems.at[CT + i]) for i in range(CT)]
    for copy in reads:
        copy.start()
    for i in range(CT):
        reads[i].wait()
        writes[i].start()
    for copy in writes:
        copy.wait()


def sort_slots(order, child):
    return pl.pallas_call(
        sort_kernel,
        out_shape=jax.ShapeDtypeStruct(child.shape, F32),
        in_specs=[pl.BlockSpec(memory_space=pltpu.SMEM), pl.BlockSpec(memory_space=pl.ANY)],
        out_specs=pl.BlockSpec(memory_space=pl.ANY),
        scratch_shapes=[pltpu.VMEM((CT, B, B), F32), pltpu.SemaphoreType.DMA((2 * CT,))],
        compiler_params=pltpu.CompilerParams(vmem_limit_bytes=32 * 2**20),
    )(order, child)


def body(front, child_tiles, child_target, child_count):
    order, meta = tables(child_target, child_count)
    child = sort_slots(order, child_tiles.reshape(CT, B, B))
    panel, updated = fused(front.reshape(ROWS, CHUNK, 1024), child, meta)
    return panel, updated.reshape(front.shape)


def solution(mesh):
    return jax.shard_map(
        body,
        mesh=mesh,
        in_specs=(
            P("row", "col"),
            P("row", "col", None, None),
            P("row", "col", None),
            P("row", "col"),
        ),
        out_specs=(P("row", None), P("row", "col")),
        check_vma=False,
    )
```
